32 devices in a mesh: space: 8 (over z, core), member: 4 (over y, x).
Axes of the slice: x: 2, y: 2, z: 4, core: 2. Of those that a mesh axis runs over, the one named last changes fastest.
Arguments:
- perturbation: float32 [4, 4, 16, 16, 1024], P('member', None, None, None, 'space'), may hold values from -6 to 6
- trajectory: bfloat16 [3, 16, 6, 16, 1024], P(None, 'member', None, None, 'space'), may hold values from -0.5 to 0.5
- site_col: int32 [8, 8, 128], P(None, 'space'), may hold values from 0 to 2047
- site_lev: int32 [8, 8, 128], P(None, 'space'), may hold values from 0 to 15
- obs_counts: int32 [8, 8], P(None, 'space'), may hold values from 0 to 128, as said below
- obs_weights: float32 [8, 8, 4, 128], P('space'), may hold values from -3 to 3
Outputs:
- final_state: float32 [4, 4, 16, 16, 1024], P('member', None, None, None, 'space')
- obs_equiv: float32 [4, 8, 8, 128], P('member', 'space')
The draws below stay inside these ranges and needn't reach their ends.
Inputs may be any that keep to these rules, and one draw needn't show every extreme that they name: obs_counts[o, s] is the number of live leading slots of owner o in tile s; some pair has exactly 128, and owners differ in load by up to four times.
All inputs are finite; a program needn't handle non-finite values.
Results may differ from the reference program's by a relative error of at most 0.0003.
Values may be sent and summed in bfloat16 or wider, within the bound.
A program may use at most 64 MiB of HBM per device.

```python
import jax
import jax.numpy as jnp
from jax import lax

L = 16
LAT = 16
LOND = 128
STEPS = 3
CAP = 128
TILES = 8
LON = 1024
MEMBERS = 4


def draw_obs_counts(key, part):
    key_heavy, key_base, key_row, key_col = jax.random.split(jax.random.fold_in(key, 17), 4)
    heavy = jax.random.randint(key_heavy, (TILES, 1), 1, 5)
    base = jax.random.randint(key_base, (TILES, TILES), 0, CAP // 3 + 1)
    counts = jnp.minimum(base * heavy, CAP)
    row = jax.random.randint(key_row, (), 0, TILES)
    column = jax.random.randint(key_col, (), 0, TILES)
    return counts.at[row, column].set(CAP).astype(jnp.int32)


def with_ends(values, rng, smallest, top_value):
    longest = values.shape.index(max(values.shape))
    spots = []
    for shift in (0, 1):
        where = [jax.random.randint(jax.random.fold_in(rng, axis), (), 0, length) for axis, length in enumerate(values.shape)]
        where[longest] = (where[longest] + shift) % values.shape[longest]
        spots.append(tuple(where))
    return values.at[spots[0]].set(smallest).at[spots[1]].set(top_value)


def steps_of(rng, shape, cuts, least, top_value):
    def one(position, blocks):
        steps = jax.random.uniform(jax.random.fold_in(jax.random.fold_in(rng, 6), position), (blocks,), jnp.float32, least / len(cuts), top_value / len(cuts))
        return jnp.repeat(jnp.exp(steps), shape[position] // blocks).reshape((-1,) + (1,) * (len(shape) - position - 1))

    gain = one(*cuts[0])
    for cut in cuts[1:]:
        gain = gain * one(*cut)
    return gain


def centred(own_key, dims, spread, limit, cuts=(), kind=jnp.bfloat16):
    array = jax.random.normal(own_key, dims, jnp.float32) * spread
    if len(cuts) > 0:
        array = steps_of(own_key, dims, cuts, -0.22, 0.18) * array
    return jnp.clip(array, min=-limit, max=limit).astype(kind)


def setup_inputs(seed: int = 0) -> dict:
    keys = jax.random.split(jax.random.key(seed), 7)
    return {
        "perturbation": centred(keys[0], (MEMBERS, 4, L, LAT, LON), 1.0, 6.0, ((0, 4), (4, 8)), jnp.float32),
        "trajectory": jnp.clip(jax.random.uniform(keys[1], (STEPS, L, 6, LAT, LON), jnp.float32, -0.5, 0.5) * steps_of(keys[1], (STEPS, L, 6, LAT, LON), ((1, 4), (4, 8)), -0.4, 0.0), -0.5, 0.5).astype(jnp.bfloat16),
        "site_col": with_ends(jax.random.randint(keys[2], (TILES, TILES, CAP), 0, LAT * LOND), jax.random.fold_in(keys[2], 1), 0, (LAT * LOND) - 1).astype(jnp.int32),
        "site_lev": with_ends(jax.random.randint(keys[3], (TILES, TILES, CAP), 0, L), jax.random.fold_in(keys[3], 1), 0, L - 1).astype(jnp.int32),
        "obs_counts": draw_obs_counts(jax.random.fold_in(keys[6], 71), 0),
        "obs_weights": centred(keys[5], (TILES, TILES, 4, CAP), 0.5, 3.0, ((0, 8),), jnp.float32),
    }


def advance(state, coef):
    east = jnp.roll(state, -1, axis=-1)
    west = jnp.roll(state, 1, axis=-1)
    padded = jnp.pad(state, ((0, 0), (0, 0), (1, 1), (0, 0)))
    north = padded[:, :, 2:, :]
    south = padded[:, :, :-2, :]
    planes = coef.astype(jnp.float32)
    along = planes[:, 0][None]
    across = planes[:, 1][None]
    fresh = state - along * (east - west) * 0.5 + 0.5 * along * along * (east - 2.0 * state + west)
    fresh = fresh - across * (north - south) * 0.5 + 0.5 * across * across * (north - 2.0 * state + south)
    wind_u = state[0]
    wind_v = state[1]
    temper = fresh[2] - (planes[:, 2] * wind_u + planes[:, 3] * wind_v)
    humid = fresh[3] - (planes[:, 4] * wind_u + planes[:, 5] * wind_v)
    return jnp.stack([fresh[0], fresh[1], temper, humid], axis=0)


def reference(perturbation, trajectory, site_col, site_lev, obs_counts, obs_weights):
    def one_member(state):
        for step in range(STEPS):
            state = advance(state, trajectory[step])
        return state

    final_state = lax.map(one_member, perturbation)
    tiles = site_col.shape[1]
    lat_idx = (site_col // LOND).astype(jnp.int32)
    source = jnp.arange(tiles, dtype=jnp.int32)[None, :, None]
    lon_idx = (source * LOND + site_col % LOND).astype(jnp.int32)
    value = final_state[:, :, site_lev, lat_idx, lon_idx]
    weights = jnp.transpose(obs_weights, (2, 0, 1, 3))[None]
    summed = jnp.sum(weights * value, axis=1)
    live = jnp.arange(CAP, dtype=jnp.int32)[None, None, :] < obs_counts[:, :, None]
    obs_equiv = jnp.where(live[None], summed, jnp.float32(0.0))
    return final_state, obs_equiv
```

```python
import functools

import jax
import jax.numpy as jnp
from jax import lax
from jax.experimental import pallas as pl
from jax.experimental.pallas import tpu as pltpu
from jax.sharding import PartitionSpec as P

MESH = pl.DeviceIdType.MESH
F32 = jnp.float32
BF16 = jnp.bfloat16
FIELDS = 4


def kernel(
    members,
    tiles,
    pert,
    traj,
    scol,
    slev,
    counts,
    weights,
    final,
    equiv,
    state,
    coef,
    halo_out,
    halo_in,
    col_v,
    lev_v,
    w_own,
    w_in,
    key_v,
    onehot,
    table,
    picked,
    obs_out,
    obs_in,
    in_sem,
    fin_sem,
    own_send,
    own_recv,
    fwd_send,
    fwd_recv,
    halo_send,
    halo_recv,
    w_send,
    w_recv,
    obs_send,
    obs_recv,
):
    nsteps, per = traj.shape[0], traj.shape[1]
    levels, rows, lanes = pert.shape[2], pert.shape[3], pert.shape[4]
    slots = scol.shape[2]
    me = lax.axis_index("member")
    tile = lax.axis_index("space")
    square = members == 4 and per % 2 == 0

    if square:
        xn = me + 1 - 2 * lax.rem(me, 2)
        yn = lax.rem(me + 2, 4)
        sources = [me, xn, yn, 3 - me]
        direct = [xn, yn]
        senders = [xn, yn]
    else:
        sources = [lax.rem(me + members - j, members) for j in range(members)]
        senders = sources[1:]
        direct = [lax.rem(me + j, members) for j in range(1, members)]
    east = lax.rem(tile + 1, tiles)
    west = lax.rem(tile + tiles - 1, tiles)
    owners = [lax.rem(tile + j, tiles) for j in range(tiles)]

    load_state = pltpu.make_async_copy(pert.at[0], state, in_sem.at[0])
    load_own = [
        pltpu.make_async_copy(traj.at[k], coef.at[k, me], in_sem.at[4 + k])
        for k in range(nsteps)
    ]
    load_col = pltpu.make_async_copy(scol, col_v, in_sem.at[1])
    load_lev = pltpu.make_async_copy(slev, lev_v, in_sem.at[2])
    load_w = pltpu.make_async_copy(weights.at[0, tile], w_in.at[tile], in_sem.at[3])
    load_state.start()
    load_own[0].start()
    load_col.start()
    load_lev.start()
    load_w.start()
    for copy in load_own[1:]:
        copy.start()

    def send_own(k, j):
        return pltpu.make_async_remote_copy(
            src_ref=traj.at[k],
            dst_ref=coef.at[k, me],
            send_sem=own_send.at[k, j],
            recv_sem=own_recv.at[k, j],
            device_id={"member": direct[j]},
            device_id_type=MESH,
        )

    def forward(k, j):
        half = per // 2
        part = coef.at[k, senders[1 - j], pl.ds(j * half, half)]
        return pltpu.make_async_remote_copy(
            src_ref=part,
            dst_ref=part,
            send_sem=fwd_send.at[k, j],
            recv_sem=fwd_recv.at[k, j],
            device_id={"member": direct[j]},
            device_id_type=MESH,
        )

    def send_halo(k, side):
        return pltpu.make_async_remote_copy(
            src_ref=halo_out.at[k],
            dst_ref=halo_in.at[k, side],
            send_sem=halo_send.at[k, side],
            recv_sem=halo_recv.at[k, side],
            device_id={"space": (east, west)[side]},
            device_id_type=MESH,
        )

    def send_w(j):
        return pltpu.make_async_remote_copy(
            src_ref=weights.at[0, owners[j]],
            dst_ref=w_in.at[tile],
            send_sem=w_send.at[j],
            recv_sem=w_recv.at[j],
            device_id={"space": owners[j]},
            device_id_type=MESH,
        )

    def send_obs(j):
        return pltpu.make_async_remote_copy(
            src_ref=obs_out.at[owners[j]],
            dst_ref=obs_in.at[tile],
            send_sem=obs_send.at[j],
            recv_sem=obs_recv.at[j],
            device_id={"space": owners[j]},
            device_id_type=MESH,
        )

    ways = range(len(direct))

    barrier = pltpu.get_barrier_semaphore()
    for peer in direct:
        pl.semaphore_signal(barrier, inc=1, device_id={"member": peer}, device_id_type=MESH)
    for j in range(1, tiles):
        pl.semaphore_signal(barrier, inc=1, device_id={"space": owners[j]}, device_id_type=MESH)
    pl.semaphore_wait(barrier, len(direct) + tiles - 1)

    for k in range(min(2, nsteps)):
        for j in ways:
            send_own(k, j).start()

    lane = lax.broadcasted_iota(jnp.int32, (rows, lanes), 1)
    row = lax.broadcasted_iota(jnp.int32, (rows, lanes), 0)
    first, last = lane == 0, lane == lanes - 1
    edge = first | last
    even = lax.rem(lane, 2) == 0

    def pack(p, q):
        kept = jnp.where(edge, p, 0.0)
        return kept if q == 0 else pltpu.roll(kept, 2 * q, 1)

    load_state.wait()
    total = None
    for c, src in enumerate(sources):
        for l in range(per):
            for f in range(FIELDS):
                term = pack(state[f, src * per + l], f * levels + c * per + l)
                total = term if total is None else total + term
    halo_out[0] = total
    for side in range(2):
        send_halo(0, side).start()
    for j in range(1, tiles):
        send_w(j).start()

    load_col.wait()
    load_lev.wait()
    lat_iota = lax.broadcasted_iota(jnp.int32, (lanes, slots), 0)
    slot_iota = lax.broadcasted_iota(jnp.int32, (1, slots), 1)
    for o in range(tiles):
        col, lev = col_v[o], lev_v[o]
        lon = lax.rem(col, lanes)
        key = lev * rows + lax.div(col, lanes)
        key_v[o] = jnp.where(slot_iota < counts[o, 0], key, -1)
        hot = jnp.where(lat_iota == lon, 1.0, 0.0).astype(BF16)
        onehot[0:lanes, o * slots : (o + 1) * slots] = hot
        onehot[lanes : 2 * lanes, o * slots : (o + 1) * slots] = hot
    picked[...] = jnp.zeros_like(picked)

    def work(k, c, halo, total):
        src = sources[c]
        for l in range(per):
            at = src * per + l
            planes = [coef[k, src, l, i].astype(F32) for i in range(6)]
            a, b = planes[0], planes[1]
            ha, hb = 0.5 * a, 0.5 * b
            aa, bb = ha * a, hb * b
            to_e, to_w = aa - ha, aa + ha
            to_n = jnp.where(row == rows - 1, 0.0, bb - hb)
            to_s = jnp.where(row == 0, 0.0, bb + hb)
            stay = 1.0 - 2.0 * (aa + bb)
            old = [state[f, at] for f in range(FIELDS)]
            for f in range(FIELDS):
                p, q = old[f], f * levels + c * per + l
                side = halo if q == 0 else pltpu.roll(halo, lanes - 2 * q, 1)
                e = jnp.where(last, side, pltpu.roll(p, lanes - 1, 1))
                w = jnp.where(first, side, pltpu.roll(p, 1, 1))
                n = pltpu.roll(p, rows - 1, 0)
                s = pltpu.roll(p, 1, 0)
                new = stay * p + (to_e * e + to_w * w) + (to_n * n + to_s * s)
                if f == 2:
                    new = new - (planes[2] * old[0] + planes[3] * old[1])
                if f == 3:
                    new = new - (planes[4] * old[0] + planes[5] * old[1])
                state[f, at] = new
                if k < nsteps - 1:
                    term = pack(new, q)
                    total = term if total is None else total + term
                else:
                    high = new.astype(BF16)
                    low = (new - high.astype(F32)).astype(BF16)
                    base = (f * per + l) * rows
                    table[base : base + rows, 0:lanes] = high
                    table[base : base + rows, lanes : 2 * lanes] = low
        return total

    def finish(c):
        src = sources[c]
        save(c).start()
        for o in range(tiles):
            vals = jnp.dot(
                table[...],
                onehot[:, o * slots : (o + 1) * slots],
                preferred_element_type=F32,
            )
            key = key_v[o]
            lat = lax.broadcasted_iota(jnp.int32, (rows, slots), 0)
            acc = picked[o]
            for l in range(per):
                some = None
                for f in range(FIELDS):
                    base = (f * per + l) * rows
                    term = w_in[o, f : f + 1, :] * vals[base : base + rows]
                    some = term if some is None else some + term
                acc = acc + jnp.where(key == lat + (src * per + l) * rows, some, 0.0)
            picked[o] = acc

    def save(c):
        span = pl.ds(sources[c] * per, per)
        return pltpu.make_async_copy(
            state.at[:, span], final.at[0, :, span], fin_sem.at[c]
        )

    def arrived(k):
        for j in ways:
            send_own(k, j).wait_recv()
            if square:
                forward(k, 1 - j).start()

    arrived(0)
    for k in range(nsteps):
        if k + 2 < nsteps:
            for j in ways:
                send_own(k + 2, j).start()
        for side in range(2):
            send_halo(k, side).wait_recv()
        halo = jnp.where(
            even,
            pltpu.roll(halo_in[k, 0], 1, 1),
            pltpu.roll(halo_in[k, 1], lanes - 1, 1),
        )
        load_own[k].wait()
        if k == nsteps - 1:
            load_w.wait()
            for j in range(1, tiles):
                send_w(j).wait_recv()
        total = None
        for c in range(len(sources)):
            if square and c == 3:
                if k + 1 < nsteps:
                    arrived(k + 1)
                for j in ways:
                    forward(k, j).wait_recv()
            total = work(k, c, halo, total)
            if k == nsteps - 1:
                finish(c)
        if not square and k + 1 < nsteps:
            arrived(k + 1)
        if k + 1 < nsteps:
            halo_out[k + 1] = total
            for side in range(2):
                send_halo(k + 1, side).start()

    for o in range(tiles):
        obs_out[o] = jnp.sum(picked[o], axis=0, keepdims=True)
    for j in range(1, tiles):
        send_obs(j).start()
    obs_in[tile] = obs_out[tile]
    for k in range(nsteps):
        for j in ways:
            send_own(k, j).wait_send()
            if square:
                forward(k, j).wait_send()
        for side in range(2):
            send_halo(k, side).wait_send()
    for j in range(1, tiles):
        send_w(j).wait_send()
    for c in range(len(sources)):
        save(c).wait()
    for j in range(1, tiles):
        send_obs(j).wait_recv()
    for o in range(tiles):
        equiv[0, 0, o : o + 1, :] = obs_in[o]
    for j in range(1, tiles):
        send_obs(j).wait_send()


def on_device(perturbation, trajectory, site_col, site_lev, obs_counts, obs_weights):
    members = lax.axis_size("member")
    tiles = lax.axis_size("space")
    nsteps, per, planes, rows, lanes = trajectory.shape
    levels = perturbation.shape[2]
    slots = site_col.shape[2]
    any_space = pl.BlockSpec(memory_space=pl.ANY)
    dma = pltpu.SemaphoreType.DMA
    near = 2 if members == 4 and per % 2 == 0 else members - 1
    return pl.pallas_call(
        functools.partial(kernel, members, tiles),
        out_shape=(
            jax.ShapeDtypeStruct(perturbation.shape, F32),
            jax.ShapeDtypeStruct((1, 1, tiles, slots), F32),
        ),
        in_specs=[any_space] * 4 + [pl.BlockSpec(memory_space=pltpu.SMEM), any_space],
        out_specs=(any_space, pl.BlockSpec(memory_space=pltpu.VMEM)),
        scratch_shapes=[
            pltpu.VMEM((FIELDS, levels, rows, lanes), F32),
            pltpu.VMEM((nsteps, members, per, planes, rows, lanes), BF16),
            pltpu.VMEM((nsteps, rows, lanes), F32),
            pltpu.VMEM((nsteps, 2, rows, lanes), F32),
            pltpu.VMEM((tiles, 1, slots), jnp.int32),
            pltpu.VMEM((tiles, 1, slots), jnp.int32),
            pltpu.VMEM((FIELDS, slots), F32),
            pltpu.VMEM((tiles, FIELDS, slots), F32),
            pltpu.VMEM((tiles, 1, slots), jnp.int32),
            pltpu.VMEM((2 * lanes, tiles * slots), BF16),
            pltpu.VMEM((FIELDS * per * rows, 2 * lanes), BF16),
            pltpu.VMEM((tiles, rows, slots), F32),
            pltpu.VMEM((tiles, 1, slots), F32),
            pltpu.VMEM((tiles, 1, slots), F32),
            dma((4 + nsteps,)),
            dma((members,)),
            dma((nsteps, near)),
            dma((nsteps, near)),
            dma((nsteps, near)),
            dma((nsteps, near)),
            dma((nsteps, 2)),
            dma((nsteps, 2)),
            dma((tiles,)),
            dma((tiles,)),
            dma((tiles,)),
            dma((tiles,)),
        ],
        compiler_params=pltpu.CompilerParams(
            collective_id=0, has_side_effects=True, vmem_limit_bytes=32 * 1024 * 1024
        ),
        name="advect_observe",
    )(perturbation, trajectory, site_col, site_lev, obs_counts, obs_weights)


def solution(mesh):
    in_specs = (
        P("member", None, None, None, "space"),
        P(None, "member", None, None, "space"),
        P(None, "space", None),
        P(None, "space", None),
        P(None, "space"),
        P("space", None, None, None),
    )
    out_specs = (P("member", None, None, None, "space"), P("member", "space", None, None))
    return jax.shard_map(
        on_device, mesh=mesh, in_specs=in_specs, out_specs=out_specs, check_vma=False
    )
```

```python
import functools

import jax
import jax.numpy as jnp
from jax import lax
from jax.experimental import pallas as pl
from jax.experimental.pallas import tpu as pltpu
from jax.sharding import PartitionSpec as P

MESH = pl.DeviceIdType.MESH
F32 = jnp.float32
BF16 = jnp.bfloat16
FIELDS = 4


def kernel(
    members,
    tiles,
    pert,
    traj,
    scol,
    slev,
    counts,
    weights,
    final,
    equiv,
    state,
    coef,
    halo_out,
    halo_in,
    col_v,
    lev_v,
    w_in,
    key_v,
    onehot,
    table,
    picked,
    obs_out,
    obs_in,
    in_sem,
    fin_sem,
    own_send,
    own_recv,
    fwd_send,
    fwd_recv,
    halo_send,
    halo_recv,
    w_send,
    w_recv,
    obs_send,
    obs_recv,
):
    nsteps, per = traj.shape[0], traj.shape[1]
    levels, rows, lanes = pert.shape[2], pert.shape[3], pert.shape[4]
    slots = scol.shape[2]
    me = lax.axis_index("member")
    tile = lax.axis_index("space")
    square = members == 4 and per % 2 == 0
    group = 2 if tiles % 2 == 0 else 1

    if square:
        xn = me + 1 - 2 * lax.rem(me, 2)
        yn = lax.rem(me + 2, 4)
        sources = [me, xn, yn, 3 - me]
        direct = [xn, yn]
        senders = [xn, yn]
    else:
        sources = [lax.rem(me + members - j, members) for j in range(members)]
        senders = sources[1:]
        direct = [lax.rem(me + j, members) for j in range(1, members)]
    east = lax.rem(tile + 1, tiles)
    west = lax.rem(tile + tiles - 1, tiles)
    owners = [lax.rem(tile + j, tiles) for j in range(tiles)]

    load_state = pltpu.make_async_copy(pert.at[0], state, in_sem.at[0])
    load_own = [
        pltpu.make_async_copy(traj.at[k], coef.at[k, me], in_sem.at[4 + k])
        for k in range(nsteps)
    ]
    load_col = pltpu.make_async_copy(scol, col_v, in_sem.at[1])
    load_lev = pltpu.make_async_copy(slev, lev_v, in_sem.at[2])
    load_w = pltpu.make_async_copy(weights.at[0, tile], w_in.at[tile], in_sem.at[3])
    load_state.start()
    load_own[0].start()
    load_col.start()
    load_lev.start()
    load_w.start()
    for copy in load_own[1:]:
        copy.start()

    def send_own(k, j):
        return pltpu.make_async_remote_copy(
            src_ref=traj.at[k],
            dst_ref=coef.at[k, me],
            send_sem=own_send.at[k, j],
            recv_sem=own_recv.at[k, j],
            device_id={"member": direct[j]},
            device_id_type=MESH,
        )

    def forward(k, j):
        half = per // 2
        part = coef.at[k, senders[1 - j], pl.ds(j * half, half)]
        return pltpu.make_async_remote_copy(
            src_ref=part,
            dst_ref=part,
            send_sem=fwd_send.at[k, j],
            recv_sem=fwd_recv.at[k, j],
            device_id={"member": direct[j]},
            device_id_type=MESH,
        )

    def send_halo(k, c, side):
        return pltpu.make_async_remote_copy(
            src_ref=halo_out.at[k, c],
            dst_ref=halo_in.at[k, c, side],
            send_sem=halo_send.at[k, c, side],
            recv_sem=halo_recv.at[k, c, side],
            device_id={"space": (east, west)[side]},
            device_id_type=MESH,
        )

    def send_w(j):
        return pltpu.make_async_remote_copy(
            src_ref=weights.at[0, owners[j]],
            dst_ref=w_in.at[tile],
            send_sem=w_send.at[j],
            recv_sem=w_recv.at[j],
            device_id={"space": owners[j]},
            device_id_type=MESH,
        )

    def send_obs(j):
        return pltpu.make_async_remote_copy(
            src_ref=obs_out.at[owners[j]],
            dst_ref=obs_in.at[tile],
            send_sem=obs_send.at[j],
            recv_sem=obs_recv.at[j],
            device_id={"space": owners[j]},
            device_id_type=MESH,
        )

    ways = range(len(direct))

    barrier = pltpu.get_barrier_semaphore()
    for peer in direct:
        pl.semaphore_signal(barrier, inc=1, device_id={"member": peer}, device_id_type=MESH)
    for j in range(1, tiles):
        pl.semaphore_signal(barrier, inc=1, device_id={"space": owners[j]}, device_id_type=MESH)
    pl.semaphore_wait(barrier, len(direct) + tiles - 1)

    for k in range(min(2, nsteps)):
        for j in ways:
            send_own(k, j).start()

    lane = lax.broadcasted_iota(jnp.int32, (rows, lanes), 1)
    row = lax.broadcasted_iota(jnp.int32, (rows, lanes), 0)
    first, last = lane == 0, lane == lanes - 1
    edge = first | last
    even = lax.rem(lane, 2) == 0

    def pack(p, q):
        kept = jnp.where(edge, p, 0.0)
        return kept if q == 0 else pltpu.roll(kept, 2 * q, 1)

    load_state.wait()
    total = None
    for c, src in enumerate(sources):
        for l in range(per):
            for f in range(FIELDS):
                term = pack(state[f, src * per + l], f * levels + c * per + l)
                total = term if total is None else total + term
    halo_out[0, 0] = total
    for side in range(2):
        send_halo(0, 0, side).start()
    for j in range(1, tiles):
        send_w(j).start()

    load_col.wait()
    load_lev.wait()
    lat_iota = lax.broadcasted_iota(jnp.int32, (lanes, slots), 0)
    slot_iota = lax.broadcasted_iota(jnp.int32, (1, slots), 1)
    for o in range(tiles):
        col, lev = col_v[o], lev_v[o]
        lon = lax.rem(col, lanes)
        key = lev * rows + lax.div(col, lanes)
        key_v[o] = jnp.where(slot_iota < counts[0, o], key, -1)
        hot = jnp.where(lat_iota == lon, 1.0, 0.0).astype(BF16)
        onehot[0:lanes, o * slots : (o + 1) * slots] = hot
        onehot[lanes : 2 * lanes, o * slots : (o + 1) * slots] = hot
    picked[...] = jnp.zeros_like(picked)

    def halo_of(k, c):
        for side in range(2):
            send_halo(k, c, side).wait_recv()
        return jnp.where(
            even,
            pltpu.roll(halo_in[k, c, 0], 1, 1),
            pltpu.roll(halo_in[k, c, 1], lanes - 1, 1),
        )

    def work(k, c):
        halo = start_halo if k == 0 else halo_of(k, c)
        total = None
        src = sources[c]
        for l in range(per):
            at = src * per + l
            planes = [coef[k, src, l, i].astype(F32) for i in range(6)]
            a, b = planes[0], planes[1]
            ha, hb = 0.5 * a, 0.5 * b
            aa, bb = ha * a, hb * b
            to_e, to_w = aa - ha, aa + ha
            to_n = jnp.where(row == rows - 1, 0.0, bb - hb)
            to_s = jnp.where(row == 0, 0.0, bb + hb)
            stay = 1.0 - 2.0 * (aa + bb)
            old = [state[f, at] for f in range(FIELDS)]
            for f in range(FIELDS):
                p, q = old[f], f * levels + c * per + l
                side = halo if q == 0 else pltpu.roll(halo, lanes - 2 * q, 1)
                e = jnp.where(last, side, pltpu.roll(p, lanes - 1, 1))
                w = jnp.where(first, side, pltpu.roll(p, 1, 1))
                n = pltpu.roll(p, rows - 1, 0)
                s = pltpu.roll(p, 1, 0)
                new = stay * p + (to_e * e + to_w * w) + (to_n * n + to_s * s)
                if f == 2:
                    new = new - (planes[2] * old[0] + planes[3] * old[1])
                if f == 3:
                    new = new - (planes[4] * old[0] + planes[5] * old[1])
                state[f, at] = new
                if k < nsteps - 1:
                    term = pack(new, q)
                    total = term if total is None else total + term
                else:
                    high = new.astype(BF16)
                    low = (new - high.astype(F32)).astype(BF16)
                    base = (f * per + l) * rows
                    table[base : base + rows, 0:lanes] = high
                    table[base : base + rows, lanes : 2 * lanes] = low
        if k < nsteps - 1:
            halo_out[k + 1, c] = total
            for side in range(2):
                send_halo(k + 1, c, side).start()
        else:
            finish(c)

    def finish(c):
        src = sources[c]
        save(c).start()
        for o in range(0, tiles, group):
            vals = jnp.dot(
                table[...],
                onehot[:, o * slots : (o + group) * slots],
                preferred_element_type=F32,
            )
            for g in range(group):
                span = slice(g * slots, (g + 1) * slots)
                key = key_v[o + g]
                acc = picked[o + g]
                for l in range(per):
                    some = None
                    for f in range(FIELDS):
                        base = (f * per + l) * rows
                        term = w_in[o + g, f : f + 1, :] * vals[base : base + rows, span]
                        some = term if some is None else some + term
                    acc = acc + jnp.where(key == row + (src * per + l) * rows, some, 0.0)
                picked[o + g] = acc

    def save(c):
        span = pl.ds(sources[c] * per, per)
        return pltpu.make_async_copy(
            state.at[:, span], final.at[0, :, span], fin_sem.at[c]
        )

    def arrived(k):
        for j in ways:
            send_own(k, j).wait_recv()
            if square:
                forward(k, 1 - j).start()

    def send_later(k):
        if k < nsteps:
            for j in ways:
                send_own(k, j).start()

    def weights_here():
        load_w.wait()
        for j in range(1, tiles):
            send_w(j).wait_recv()

    def forwarded(k):
        for j in ways:
            forward(k, j).wait_recv()

    start_halo = halo_of(0, 0)
    load_own[0].wait()
    work(0, 0)
    if square and nsteps == 3:
        arrived(0)
        send_later(2)
        work(0, 1)
        work(0, 2)
        load_own[1].wait()
        work(1, 0)
        arrived(1)
        work(1, 1)
        work(1, 2)
        forwarded(0)
        work(0, 3)
        load_own[2].wait()
        arrived(2)
        weights_here()
        work(2, 0)
        forwarded(1)
        work(1, 3)
        work(2, 1)
        work(2, 2)
        forwarded(2)
        work(2, 3)
    else:
        for k in range(nsteps):
            arrived(k)
            send_later(k + 2)
            if k > 0:
                load_own[k].wait()
            if k == nsteps - 1:
                weights_here()
            if square:
                forwarded(k)
            for c in range(1 if k == 0 else 0, len(sources)):
                work(k, c)

    for o in range(tiles):
        obs_out[o] = jnp.sum(picked[o], axis=0, keepdims=True)
    for j in range(1, tiles):
        send_obs(j).start()
    obs_in[tile] = obs_out[tile]
    for k in range(nsteps):
        for j in ways:
            send_own(k, j).wait_send()
            if square:
                forward(k, j).wait_send()
        for c in range(1 if k == 0 else len(sources)):
            for side in range(2):
                send_halo(k, c, side).wait_send()
    for j in range(1, tiles):
        send_w(j).wait_send()
    for c in range(len(sources)):
        save(c).wait()
    for j in range(1, tiles):
        send_obs(j).wait_recv()
    for o in range(tiles):
        equiv[0, 0, o : o + 1, :] = obs_in[o]
    for j in range(1, tiles):
        send_obs(j).wait_send()


def hand_over(state, equiv, state_out, equiv_out, sem):
    copies = [
        pltpu.make_async_copy(state, state_out, sem.at[0]),
        pltpu.make_async_copy(equiv, equiv_out, sem.at[1]),
    ]
    for copy in copies:
        copy.start()
    for copy in copies:
        copy.wait()


def on_device(perturbation, trajectory, site_col, site_lev, obs_counts, obs_weights):
    members = lax.axis_size("member")
    tiles = lax.axis_size("space")
    nsteps, per, planes, rows, lanes = trajectory.shape
    levels = perturbation.shape[2]
    slots = site_col.shape[2]
    any_space = pl.BlockSpec(memory_space=pl.ANY)
    hbm = pl.BlockSpec(memory_space=pltpu.HBM)
    dma = pltpu.SemaphoreType.DMA
    near = 2 if members == 4 and per % 2 == 0 else members - 1
    outs = pl.pallas_call(
        functools.partial(kernel, members, tiles),
        out_shape=(
            jax.ShapeDtypeStruct(perturbation.shape, F32),
            jax.ShapeDtypeStruct((1, 1, tiles, slots), F32),
        ),
        in_specs=[hbm] * 4 + [pl.BlockSpec(memory_space=pltpu.SMEM), hbm],
        out_specs=(any_space, pl.BlockSpec(memory_space=pltpu.VMEM)),
        scratch_shapes=[
            pltpu.VMEM((FIELDS, levels, rows, lanes), F32),
            pltpu.VMEM((nsteps, members, per, planes, rows, lanes), BF16),
            pltpu.VMEM((nsteps, members, rows, lanes), F32),
            pltpu.VMEM((nsteps, members, 2, rows, lanes), F32),
            pltpu.VMEM((tiles, 1, slots), jnp.int32),
            pltpu.VMEM((tiles, 1, slots), jnp.int32),
            pltpu.VMEM((tiles, FIELDS, slots), F32),
            pltpu.VMEM((tiles, 1, slots), jnp.int32),
            pltpu.VMEM((2 * lanes, tiles * slots), BF16),
            pltpu.VMEM((FIELDS * per * rows, 2 * lanes), BF16),
            pltpu.VMEM((tiles, rows, slots), F32),
            pltpu.VMEM((tiles, 1, slots), F32),
            pltpu.VMEM((tiles, 1, slots), F32),
            dma((4 + nsteps,)),
            dma((members,)),
            dma((nsteps, near)),
            dma((nsteps, near)),
            dma((nsteps, near)),
            dma((nsteps, near)),
            dma((nsteps, members, 2)),
            dma((nsteps, members, 2)),
            dma((tiles,)),
            dma((tiles,)),
            dma((tiles,)),
            dma((tiles,)),
        ],
        compiler_params=pltpu.CompilerParams(
            collective_id=0, has_side_effects=True, vmem_limit_bytes=60 * 1024 * 1024
        ),
        name="advect_observe",
    )(
        perturbation,
        trajectory,
        site_col,
        site_lev,
        obs_counts.reshape(1, tiles),
        obs_weights,
    )
    return pl.pallas_call(
        hand_over,
        out_shape=tuple(jax.ShapeDtypeStruct(x.shape, x.dtype) for x in outs),
        in_specs=[any_space] * 2,
        out_specs=(hbm, hbm),
        scratch_shapes=[dma((2,))],
        compiler_params=pltpu.CompilerParams(vmem_limit_bytes=60 * 1024 * 1024),
        name="hand_over",
    )(*outs)


def solution(mesh):
    in_specs = (
        P("member", None, None, None, "space"),
        P(None, "member", None, None, "space"),
        P(None, "space", None),
        P(None, "space", None),
        P(None, "space"),
        P("space", None, None, None),
    )
    out_specs = (P("member", None, None, None, "space"), P("member", "space", None, None))
    return jax.shard_map(
        on_device, mesh=mesh, in_specs=in_specs, out_specs=out_specs, check_vma=False
    )
```

```python
import functools

import jax
import jax.numpy as jnp
from jax import lax
from jax.experimental import pallas as pl
from jax.experimental.pallas import tpu as pltpu
from jax.sharding import PartitionSpec as P

MESH = pl.DeviceIdType.MESH
F32 = jnp.float32
BF16 = jnp.bfloat16
FIELDS = 4


def kernel(
    members,
    tiles,
    pert,
    traj,
    scol,
    slev,
    counts,
    weights,
    state,
    equiv,
    coef,
    halo_out,
    halo_in,
    col_v,
    lev_v,
    w_in,
    key_v,
    onehot,
    table,
    picked,
    obs_out,
    obs_in,
    in_sem,
    own_send,
    own_recv,
    fwd_send,
    fwd_recv,
    halo_send,
    halo_recv,
    w_send,
    w_recv,
    obs_send,
    obs_recv,
):
    nsteps, per = traj.shape[0], traj.shape[1]
    levels, rows, lanes = pert.shape[2], pert.shape[3], pert.shape[4]
    slots = scol.shape[2]
    me = lax.axis_index("member")
    tile = lax.axis_index("space")
    square = members == 4 and per % 2 == 0
    group = 2 if tiles % 2 == 0 else 1

    if square:
        xn = me + 1 - 2 * lax.rem(me, 2)
        yn = lax.rem(me + 2, 4)
        sources = [me, xn, yn, 3 - me]
        direct = [xn, yn]
        senders = [xn, yn]
    else:
        sources = [lax.rem(me + members - j, members) for j in range(members)]
        senders = sources[1:]
        direct = [lax.rem(me + j, members) for j in range(1, members)]
    east = lax.rem(tile + 1, tiles)
    west = lax.rem(tile + tiles - 1, tiles)
    owners = [lax.rem(tile + j, tiles) for j in range(tiles)]

    load_state = pltpu.make_async_copy(pert, state, in_sem.at[0])
    load_own = [
        pltpu.make_async_copy(traj.at[k], coef.at[k, me], in_sem.at[4 + k])
        for k in range(nsteps)
    ]
    load_col = pltpu.make_async_copy(scol, col_v, in_sem.at[1])
    load_lev = pltpu.make_async_copy(slev, lev_v, in_sem.at[2])
    load_w = pltpu.make_async_copy(weights.at[0, tile], w_in.at[tile], in_sem.at[3])
    load_state.start()
    load_own[0].start()
    load_col.start()
    load_lev.start()
    load_w.start()
    for copy in load_own[1:]:
        copy.start()

    parts = 2 if square else 1
    size = per // parts

    def send_own(k, j, h):
        return pltpu.make_async_remote_copy(
            src_ref=traj.at[k, pl.ds(h * size, size)],
            dst_ref=coef.at[k, me, pl.ds(h * size, size)],
            send_sem=own_send.at[k, j, h],
            recv_sem=own_recv.at[k, j, h],
            device_id={"member": direct[j]},
            device_id_type=MESH,
        )

    def forward(k, j):
        part = coef.at[k, senders[1 - j], pl.ds(j * size, size)]
        return pltpu.make_async_remote_copy(
            src_ref=part,
            dst_ref=part,
            send_sem=fwd_send.at[k, j],
            recv_sem=fwd_recv.at[k, j],
            device_id={"member": direct[j]},
            device_id_type=MESH,
        )

    def send_halo(k, c, side):
        return pltpu.make_async_remote_copy(
            src_ref=halo_out.at[k, c],
            dst_ref=halo_in.at[k, c, side],
            send_sem=halo_send.at[k, c, side],
            recv_sem=halo_recv.at[k, c, side],
            device_id={"space": (east, west)[side]},
            device_id_type=MESH,
        )

    def send_w(j):
        return pltpu.make_async_remote_copy(
            src_ref=weights.at[0, owners[j]],
            dst_ref=w_in.at[tile],
            send_sem=w_send.at[j],
            recv_sem=w_recv.at[j],
            device_id={"space": owners[j]},
            device_id_type=MESH,
        )

    def send_obs(j):
        return pltpu.make_async_remote_copy(
            src_ref=obs_out.at[owners[j]],
            dst_ref=obs_in.at[tile],
            send_sem=obs_send.at[j],
            recv_sem=obs_recv.at[j],
            device_id={"space": owners[j]},
            device_id_type=MESH,
        )

    ways = range(len(direct))

    barrier = pltpu.get_barrier_semaphore()
    for peer in direct:
        pl.semaphore_signal(barrier, inc=1, device_id={"member": peer}, device_id_type=MESH)
    for j in range(1, tiles):
        pl.semaphore_signal(barrier, inc=1, device_id={"space": owners[j]}, device_id_type=MESH)
    pl.semaphore_wait(barrier, len(direct) + tiles - 1)

    def send_slab(k):
        if k < nsteps:
            for h in range(parts):
                for j in ways:
                    send_own(k, j, (h + 1 - j) % parts).start()

    send_slab(0)
    send_slab(1)

    lane = lax.broadcasted_iota(jnp.int32, (rows, lanes), 1)
    row = lax.broadcasted_iota(jnp.int32, (rows, lanes), 0)
    first, last = lane == 0, lane == lanes - 1
    edge = first | last
    even = lax.rem(lane, 2) == 0

    def pack(p, q):
        kept = jnp.where(edge, p, 0.0)
        return kept if q == 0 else pltpu.roll(kept, 2 * q, 1)

    load_state.wait()
    total = None
    for c, src in enumerate(sources):
        for l in range(per):
            for f in range(FIELDS):
                term = pack(state[0, f, src * per + l], f * levels + c * per + l)
                total = term if total is None else total + term
    halo_out[0, 0] = total
    for side in range(2):
        send_halo(0, 0, side).start()
    for j in range(1, tiles):
        send_w(j).start()

    load_col.wait()
    load_lev.wait()
    lat_iota = lax.broadcasted_iota(jnp.int32, (lanes, slots), 0)
    slot_iota = lax.broadcasted_iota(jnp.int32, (1, slots), 1)
    for o in range(tiles):
        col, lev = col_v[o], lev_v[o]
        lon = lax.rem(col, lanes)
        key = lev * rows + lax.div(col, lanes)
        key_v[o] = jnp.where(slot_iota < counts[0, o], key, -1)
        hot = jnp.where(lat_iota == lon, 1.0, 0.0).astype(BF16)
        onehot[0:lanes, o * slots : (o + 1) * slots] = hot
        onehot[lanes : 2 * lanes, o * slots : (o + 1) * slots] = hot
    picked[...] = jnp.zeros_like(picked)

    def halo_of(k, c):
        for side in range(2):
            send_halo(k, c, side).wait_recv()
        return jnp.where(
            even,
            pltpu.roll(halo_in[k, c, 0], 1, 1),
            pltpu.roll(halo_in[k, c, 1], lanes - 1, 1),
        )

    def work(k, c):
        halo = start_halo if k == 0 else halo_of(k, c)
        total = None
        src = sources[c]
        for l in range(per):
            at = src * per + l
            planes = [coef[k, src, l, i].astype(F32) for i in range(6)]
            a, b = planes[0], planes[1]
            ha, hb = 0.5 * a, 0.5 * b
            aa, bb = ha * a, hb * b
            to_e, to_w = aa - ha, aa + ha
            to_n = jnp.where(row == rows - 1, 0.0, bb - hb)
            to_s = jnp.where(row == 0, 0.0, bb + hb)
            stay = 1.0 - 2.0 * (aa + bb)
            old = [state[0, f, at] for f in range(FIELDS)]
            for f in range(FIELDS):
                p, q = old[f], f * levels + c * per + l
                side = halo if q == 0 else pltpu.roll(halo, lanes - 2 * q, 1)
                e = jnp.where(last, side, pltpu.roll(p, lanes - 1, 1))
                w = jnp.where(first, side, pltpu.roll(p, 1, 1))
                n = pltpu.roll(p, rows - 1, 0)
                s = pltpu.roll(p, 1, 0)
                new = stay * p + (to_e * e + to_w * w) + (to_n * n + to_s * s)
                if f == 2:
                    new = new - (planes[2] * old[0] + planes[3] * old[1])
                if f == 3:
                    new = new - (planes[4] * old[0] + planes[5] * old[1])
                state[0, f, at] = new
                if k < nsteps - 1:
                    term = pack(new, q)
                    total = term if total is None else total + term
                else:
                    high = new.astype(BF16)
                    low = (new - high.astype(F32)).astype(BF16)
                    base = (f * per + l) * rows
                    table[base : base + rows, 0:lanes] = high
                    table[base : base + rows, lanes : 2 * lanes] = low
        if k < nsteps - 1:
            halo_out[k + 1, c] = total
            for side in range(2):
                send_halo(k + 1, c, side).start()
        else:
            finish(c)

    def finish(c):
        src = sources[c]
        for o in range(0, tiles, group):
            vals = jnp.dot(
                table[...],
                onehot[:, o * slots : (o + group) * slots],
                preferred_element_type=F32,
            )
            for g in range(group):
                span = slice(g * slots, (g + 1) * slots)
                key = key_v[o + g]
                acc = picked[o + g]
                for l in range(per):
                    some = None
                    for f in range(FIELDS):
                        base = (f * per + l) * rows
                        term = w_in[o + g, f : f + 1, :] * vals[base : base + rows, span]
                        some = term if some is None else some + term
                    acc = acc + jnp.where(key == row + (src * per + l) * rows, some, 0.0)
                picked[o + g] = acc

    def pass_on(k):
        if square:
            for j in ways:
                send_own(k, j, 1 - j).wait_recv()
                forward(k, 1 - j).start()

    def arrived(k):
        for j in ways:
            for h in range(parts):
                if not square or h == j:
                    send_own(k, j, h).wait_recv()

    def weights_here():
        load_w.wait()
        for j in range(1, tiles):
            send_w(j).wait_recv()

    def forwarded(k):
        for j in ways:
            forward(k, j).wait_recv()

    start_halo = halo_of(0, 0)
    load_own[0].wait()
    work(0, 0)
    if square and nsteps == 3:
        pass_on(0)
        send_slab(2)
        arrived(0)
        work(0, 1)
        work(0, 2)
        load_own[1].wait()
        work(1, 0)
        pass_on(1)
        arrived(1)
        work(1, 1)
        work(1, 2)
        forwarded(0)
        work(0, 3)
        load_own[2].wait()
        pass_on(2)
        weights_here()
        work(2, 0)
        forwarded(1)
        work(1, 3)
        arrived(2)
        work(2, 1)
        work(2, 2)
        forwarded(2)
        work(2, 3)
    else:
        for k in range(nsteps):
            pass_on(k)
            send_slab(k + 2)
            arrived(k)
            if k > 0:
                load_own[k].wait()
            if k == nsteps - 1:
                weights_here()
            if square:
                forwarded(k)
            for c in range(1 if k == 0 else 0, len(sources)):
                work(k, c)

    for o in range(tiles):
        obs_out[o] = jnp.sum(picked[o], axis=0, keepdims=True)
    for j in range(1, tiles):
        send_obs(j).start()
    obs_in[tile] = obs_out[tile]
    for k in range(nsteps):
        for j in ways:
            for h in range(parts):
                send_own(k, j, h).wait_send()
            if square:
                forward(k, j).wait_send()
        for c in range(1 if k == 0 else len(sources)):
            for side in range(2):
                send_halo(k, c, side).wait_send()
    for j in range(1, tiles):
        send_w(j).wait_send()
    for j in range(1, tiles):
        send_obs(j).wait_recv()
    for o in range(tiles):
        equiv[0, 0, o : o + 1, :] = obs_in[o]
    for j in range(1, tiles):
        send_obs(j).wait_send()


def on_device(perturbation, trajectory, site_col, site_lev, obs_counts, obs_weights):
    members = lax.axis_size("member")
    tiles = lax.axis_size("space")
    nsteps, per, planes, rows, lanes = trajectory.shape
    levels = perturbation.shape[2]
    slots = site_col.shape[2]
    hbm = pl.BlockSpec(memory_space=pltpu.HBM)
    dma = pltpu.SemaphoreType.DMA
    near = 2 if members == 4 and per % 2 == 0 else members - 1
    return pl.pallas_call(
        functools.partial(kernel, members, tiles),
        out_shape=(
            pltpu.VMEM(perturbation.shape, F32),
            pltpu.VMEM((1, 1, tiles, slots), F32),
        ),
        in_specs=[hbm] * 4 + [pl.BlockSpec(memory_space=pltpu.SMEM), hbm],
        out_specs=(pl.BlockSpec(memory_space=pltpu.VMEM),) * 2,
        scratch_shapes=[
            pltpu.VMEM((nsteps, members, per, planes, rows, lanes), BF16),
            pltpu.VMEM((nsteps, members, rows, lanes), F32),
            pltpu.VMEM((nsteps, members, 2, rows, lanes), F32),
            pltpu.VMEM((tiles, 1, slots), jnp.int32),
            pltpu.VMEM((tiles, 1, slots), jnp.int32),
            pltpu.VMEM((tiles, FIELDS, slots), F32),
            pltpu.VMEM((tiles, 1, slots), jnp.int32),
            pltpu.VMEM((2 * lanes, tiles * slots), BF16),
            pltpu.VMEM((FIELDS * per * rows, 2 * lanes), BF16),
            pltpu.VMEM((tiles, rows, slots), F32),
            pltpu.VMEM((tiles, 1, slots), F32),
            pltpu.VMEM((tiles, 1, slots), F32),
            dma((4 + nsteps,)),
            dma((nsteps, near, 2)),
            dma((nsteps, near, 2)),
            dma((nsteps, near)),
            dma((nsteps, near)),
            dma((nsteps, members, 2)),
            dma((nsteps, members, 2)),
            dma((tiles,)),
            dma((tiles,)),
            dma((tiles,)),
            dma((tiles,)),
        ],
        compiler_params=pltpu.CompilerParams(
            collective_id=0, has_side_effects=True, vmem_limit_bytes=60 * 1024 * 1024
        ),
        name="advect_observe",
    )(
        perturbation,
        trajectory,
        site_col,
        site_lev,
        obs_counts.reshape(1, tiles),
        obs_weights,
    )


def solution(mesh):
    in_specs = (
        P("member", None, None, None, "space"),
        P(None, "member", None, None, "space"),
        P(None, "space", None),
        P(None, "space", None),
        P(None, "space"),
        P("space", None, None, None),
    )
    out_specs = (P("member", None, None, None, "space"), P("member", "space", None, None))
    return jax.shard_map(
        on_device, mesh=mesh, in_specs=in_specs, out_specs=out_specs, check_vma=False
    )
```

```python
import functools

import jax
import jax.numpy as jnp
from jax import lax
from jax.experimental import pallas as pl
from jax.experimental.pallas import tpu as pltpu
from jax.sharding import PartitionSpec as P

MESH = pl.DeviceIdType.MESH
F32 = jnp.float32
BF16 = jnp.bfloat16
FIELDS = 4


def kernel(
    members,
    tiles,
    pert,
    traj,
    scol,
    slev,
    counts,
    weights,
    state,
    equiv,
    coef,
    halo_out,
    halo_in,
    col_v,
    lev_v,
    w_in,
    key_v,
    onehot,
    table,
    picked,
    obs_out,
    obs_in,
    in_sem,
    own_send,
    own_recv,
    fwd_send,
    fwd_recv,
    halo_send,
    halo_recv,
    w_send,
    w_recv,
    obs_send,
    obs_recv,
):
    nsteps, per = traj.shape[0], traj.shape[1]
    levels, rows, lanes = pert.shape[2], pert.shape[3], pert.shape[4]
    slots = scol.shape[2]
    me = lax.axis_index("member")
    tile = lax.axis_index("space")
    square = members == 4 and per % 2 == 0
    group = 2 if tiles % 2 == 0 else 1

    if square:
        xn = me + 1 - 2 * lax.rem(me, 2)
        yn = lax.rem(me + 2, 4)
        sources = [me, xn, yn, 3 - me]
        direct = [xn, yn]
        senders = [xn, yn]
    else:
        sources = [lax.rem(me + members - j, members) for j in range(members)]
        senders = sources[1:]
        direct = [lax.rem(me + j, members) for j in range(1, members)]
    east = lax.rem(tile + 1, tiles)
    west = lax.rem(tile + tiles - 1, tiles)
    owners = [lax.rem(tile + j, tiles) for j in range(tiles)]

    load_state = pltpu.make_async_copy(pert, state, in_sem.at[0])
    load_own = [
        pltpu.make_async_copy(traj.at[k], coef.at[k, me], in_sem.at[4 + k])
        for k in range(nsteps)
    ]
    load_col = pltpu.make_async_copy(scol, col_v, in_sem.at[1])
    load_lev = pltpu.make_async_copy(slev, lev_v, in_sem.at[2])
    load_w = pltpu.make_async_copy(weights.at[0, tile], w_in.at[tile], in_sem.at[3])
    load_state.start()
    load_own[0].start()
    load_col.start()
    load_lev.start()
    load_w.start()
    for copy in load_own[1:]:
        copy.start()

    parts = 2 if square else 1
    size = per // parts

    def send_own(k, j, h):
        return pltpu.make_async_remote_copy(
            src_ref=traj.at[k, pl.ds(h * size, size)],
            dst_ref=coef.at[k, me, pl.ds(h * size, size)],
            send_sem=own_send.at[k, j, h],
            recv_sem=own_recv.at[k, j, h],
            device_id={"member": direct[j]},
            device_id_type=MESH,
        )

    def forward(k, j):
        part = coef.at[k, senders[1 - j], pl.ds(j * size, size)]
        return pltpu.make_async_remote_copy(
            src_ref=part,
            dst_ref=part,
            send_sem=fwd_send.at[k, j],
            recv_sem=fwd_recv.at[k, j],
            device_id={"member": direct[j]},
            device_id_type=MESH,
        )

    def send_halo(k, c, side):
        return pltpu.make_async_remote_copy(
            src_ref=halo_out.at[k, c],
            dst_ref=halo_in.at[k, c, side],
            send_sem=halo_send.at[k, c, side],
            recv_sem=halo_recv.at[k, c, side],
            device_id={"space": (east, west)[side]},
            device_id_type=MESH,
        )

    def send_w(j):
        return pltpu.make_async_remote_copy(
            src_ref=weights.at[0, owners[j]],
            dst_ref=w_in.at[tile],
            send_sem=w_send.at[j],
            recv_sem=w_recv.at[j],
            device_id={"space": owners[j]},
            device_id_type=MESH,
        )

    def send_obs(j):
        return pltpu.make_async_remote_copy(
            src_ref=obs_out.at[owners[j]],
            dst_ref=obs_in.at[tile],
            send_sem=obs_send.at[j],
            recv_sem=obs_recv.at[j],
            device_id={"space": owners[j]},
            device_id_type=MESH,
        )

    ways = range(len(direct))

    barrier = pltpu.get_barrier_semaphore()
    for peer in direct:
        pl.semaphore_signal(barrier, inc=1, device_id={"member": peer}, device_id_type=MESH)
    for j in range(1, tiles):
        pl.semaphore_signal(barrier, inc=1, device_id={"space": owners[j]}, device_id_type=MESH)
    pl.semaphore_wait(barrier, len(direct) + tiles - 1)

    def send_slab(k, halves=range(parts)):
        if k < nsteps:
            for h in halves:
                for j in ways:
                    send_own(k, j, (h + 1 - j) % parts).start()

    staged = square and nsteps == 3
    send_slab(0)
    if not staged:
        send_slab(1)

    lane = lax.broadcasted_iota(jnp.int32, (rows, lanes), 1)
    row = lax.broadcasted_iota(jnp.int32, (rows, lanes), 0)
    first, last = lane == 0, lane == lanes - 1
    edge = first | last
    even = lax.rem(lane, 2) == 0

    def pack(p, q):
        kept = jnp.where(edge, p, 0.0)
        return kept if q == 0 else pltpu.roll(kept, 2 * q, 1)

    load_state.wait()
    total = None
    for c, src in enumerate(sources):
        for l in range(per):
            for f in range(FIELDS):
                term = pack(state[0, f, src * per + l], f * levels + c * per + l)
                total = term if total is None else total + term
    halo_out[0, 0] = total
    for side in range(2):
        send_halo(0, 0, side).start()
    for j in range(1, tiles):
        send_w(j).start()

    def pass_on(k):
        if square:
            for j in ways:
                send_own(k, j, 1 - j).wait_recv()
                forward(k, 1 - j).start()

    def arrived(k):
        for j in ways:
            for h in range(parts):
                if not square or h == j:
                    send_own(k, j, h).wait_recv()

    if staged:
        pass_on(0)
        send_slab(1)
        send_slab(2, [0])

    load_col.wait()
    load_lev.wait()
    lat_iota = lax.broadcasted_iota(jnp.int32, (lanes, slots), 0)
    slot_iota = lax.broadcasted_iota(jnp.int32, (1, slots), 1)
    for o in range(tiles):
        col, lev = col_v[o], lev_v[o]
        lon = lax.rem(col, lanes)
        key = lev * rows + lax.div(col, lanes)
        key_v[o] = jnp.where(slot_iota < counts[0, o], key, -1)
        hot = jnp.where(lat_iota == lon, 1.0, 0.0).astype(BF16)
        onehot[0:lanes, o * slots : (o + 1) * slots] = hot
        onehot[lanes : 2 * lanes, o * slots : (o + 1) * slots] = hot
    picked[...] = jnp.zeros_like(picked)

    def halo_of(k, c):
        for side in range(2):
            send_halo(k, c, side).wait_recv()
        return jnp.where(
            even,
            pltpu.roll(halo_in[k, c, 0], 1, 1),
            pltpu.roll(halo_in[k, c, 1], lanes - 1, 1),
        )

    def work(k, c):
        halo = start_halo if k == 0 else halo_of(k, c)
        total = None
        src = sources[c]
        for l in range(per):
            at = src * per + l
            planes = [coef[k, src, l, i].astype(F32) for i in range(6)]
            a, b = planes[0], planes[1]
            ha, hb = 0.5 * a, 0.5 * b
            aa, bb = ha * a, hb * b
            to_e, to_w = aa - ha, aa + ha
            to_n = jnp.where(row == rows - 1, 0.0, bb - hb)
            to_s = jnp.where(row == 0, 0.0, bb + hb)
            stay = 1.0 - 2.0 * (aa + bb)
            old = [state[0, f, at] for f in range(FIELDS)]
            for f in range(FIELDS):
                p, q = old[f], f * levels + c * per + l
                side = halo if q == 0 else pltpu.roll(halo, lanes - 2 * q, 1)
                e = jnp.where(last, side, pltpu.roll(p, lanes - 1, 1))
                w = jnp.where(first, side, pltpu.roll(p, 1, 1))
                n = pltpu.roll(p, rows - 1, 0)
                s = pltpu.roll(p, 1, 0)
                new = stay * p + (to_e * e + to_w * w) + (to_n * n + to_s * s)
                if f == 2:
                    new = new - (planes[2] * old[0] + planes[3] * old[1])
                if f == 3:
                    new = new - (planes[4] * old[0] + planes[5] * old[1])
                state[0, f, at] = new
                if k < nsteps - 1:
                    term = pack(new, q)
                    total = term if total is None else total + term
                else:
                    high = new.astype(BF16)
                    low = (new - high.astype(F32)).astype(BF16)
                    base = (f * per + l) * rows
                    table[base : base + rows, 0:lanes] = high
                    table[base : base + rows, lanes : 2 * lanes] = low
        if k < nsteps - 1:
            halo_out[k + 1, c] = total
            for side in range(2):
                send_halo(k + 1, c, side).start()
        else:
            finish(c)

    def finish(c):
        src = sources[c]
        for o in range(0, tiles, group):
            vals = jnp.dot(
                table[...],
                onehot[:, o * slots : (o + group) * slots],
                preferred_element_type=F32,
            )
            for g in range(group):
                span = slice(g * slots, (g + 1) * slots)
                key = key_v[o + g]
                acc = picked[o + g]
                for l in range(per):
                    some = None
                    for f in range(FIELDS):
                        base = (f * per + l) * rows
                        term = w_in[o + g, f : f + 1, :] * vals[base : base + rows, span]
                        some = term if some is None else some + term
                    acc = acc + jnp.where(key == row + (src * per + l) * rows, some, 0.0)
                picked[o + g] = acc

    def weights_here():
        load_w.wait()
        for j in range(1, tiles):
            send_w(j).wait_recv()

    def forwarded(k):
        for j in ways:
            forward(k, j).wait_recv()

    start_halo = halo_of(0, 0)
    load_own[0].wait()
    work(0, 0)
    if staged:
        arrived(0)
        work(0, 1)
        work(0, 2)
        forwarded(0)
        work(0, 3)
        pass_on(1)
        send_slab(2, [1])
        load_own[1].wait()
        work(1, 0)
        arrived(1)
        work(1, 1)
        pass_on(2)
        work(1, 2)
        forwarded(1)
        work(1, 3)
        load_own[2].wait()
        weights_here()
        work(2, 0)
        arrived(2)
        work(2, 1)
        work(2, 2)
        forwarded(2)
        work(2, 3)
    else:
        for k in range(nsteps):
            pass_on(k)
            send_slab(k + 2)
            arrived(k)
            if k > 0:
                load_own[k].wait()
            if k == nsteps - 1:
                weights_here()
            if square:
                forwarded(k)
            for c in range(1 if k == 0 else 0, len(sources)):
                work(k, c)

    for o in range(tiles):
        obs_out[o] = jnp.sum(picked[o], axis=0, keepdims=True)
    for j in range(1, tiles):
        send_obs(j).start()
    obs_in[tile] = obs_out[tile]
    for k in range(nsteps):
        for j in ways:
            for h in range(parts):
                send_own(k, j, h).wait_send()
            if square:
                forward(k, j).wait_send()
        for c in range(1 if k == 0 else len(sources)):
            for side in range(2):
                send_halo(k, c, side).wait_send()
    for j in range(1, tiles):
        send_w(j).wait_send()
    for j in range(1, tiles):
        send_obs(j).wait_recv()
    for o in range(tiles):
        equiv[0, 0, o : o + 1, :] = obs_in[o]
    for j in range(1, tiles):
        send_obs(j).wait_send()


def on_device(perturbation, trajectory, site_col, site_lev, obs_counts, obs_weights):
    members = lax.axis_size("member")
    tiles = lax.axis_size("space")
    nsteps, per, planes, rows, lanes = trajectory.shape
    levels = perturbation.shape[2]
    slots = site_col.shape[2]
    hbm = pl.BlockSpec(memory_space=pltpu.HBM)
    dma = pltpu.SemaphoreType.DMA
    near = 2 if members == 4 and per % 2 == 0 else members - 1
    return pl.pallas_call(
        functools.partial(kernel, members, tiles),
        out_shape=(
            pltpu.VMEM(perturbation.shape, F32),
            pltpu.VMEM((1, 1, tiles, slots), F32),
        ),
        in_specs=[hbm] * 4 + [pl.BlockSpec(memory_space=pltpu.SMEM), hbm],
        out_specs=(pl.BlockSpec(memory_space=pltpu.VMEM),) * 2,
        scratch_shapes=[
            pltpu.VMEM((nsteps, members, per, planes, rows, lanes), BF16),
            pltpu.VMEM((nsteps, members, rows, lanes), F32),
            pltpu.VMEM((nsteps, members, 2, rows, lanes), F32),
            pltpu.VMEM((tiles, 1, slots), jnp.int32),
            pltpu.VMEM((tiles, 1, slots), jnp.int32),
            pltpu.VMEM((tiles, FIELDS, slots), F32),
            pltpu.VMEM((tiles, 1, slots), jnp.int32),
            pltpu.VMEM((2 * lanes, tiles * slots), BF16),
            pltpu.VMEM((FIELDS * per * rows, 2 * lanes), BF16),
            pltpu.VMEM((tiles, rows, slots), F32),
            pltpu.VMEM((tiles, 1, slots), F32),
            pltpu.VMEM((tiles, 1, slots), F32),
            dma((4 + nsteps,)),
            dma((nsteps, near, 2)),
            dma((nsteps, near, 2)),
            dma((nsteps, near)),
            dma((nsteps, near)),
            dma((nsteps, members, 2)),
            dma((nsteps, members, 2)),
            dma((tiles,)),
            dma((tiles,)),
            dma((tiles,)),
            dma((tiles,)),
        ],
        compiler_params=pltpu.CompilerParams(
            collective_id=0, has_side_effects=True, vmem_limit_bytes=60 * 1024 * 1024
        ),
        name="advect_observe",
    )(
        perturbation,
        trajectory,
        site_col,
        site_lev,
        obs_counts.reshape(1, tiles),
        obs_weights,
    )


def solution(mesh):
    in_specs = (
        P("member", None, None, None, "space"),
        P(None, "member", None, None, "space"),
        P(None, "space", None),
        P(None, "space", None),
        P(None, "space"),
        P("space", None, None, None),
    )
    out_specs = (P("member", None, None, None, "space"), P("member", "space", None, None))
    return jax.shard_map(
        on_device, mesh=mesh, in_specs=in_specs, out_specs=out_specs, check_vma=False
    )
```
